32 devices in a mesh: orient: 32 (over z, y, x, core), slab: 1.
Axes of the slice: x: 2, y: 2, z: 4, core: 2. Of those that a mesh axis runs over, the one named last changes fastest.
Arguments:
- volume: bfloat16 [32, 128, 8192], P('orient', 'slab'), may hold values from 0 to 2
- rays: bfloat16 [8192, 8, 128], replicated, may hold values from -0.0234375 to 0.0234375
- band_start: int32 [8, 32], P(None, 'orient'), may hold values from 0 to 63
- band_len: int32 [8, 32], P(None, 'orient'), may hold values from 32 to 64
- slot_image: int32 [32], replicated, may hold values from 0 to 31, each once
- measured: float32 [32, 128, 128], P('orient', 'slab'), may hold values from -6 to 6
- relax: float32 [32], P('orient'), may hold values from 0.25 to 1
Outputs:
- updated: bfloat16 [32, 128, 8192], P('orient', 'slab')
- residual: float32 [32, 128, 128], P('orient', 'slab')
The draws below stay inside these ranges and needn't reach their ends.
Inputs may be any that keep to these rules, and one draw needn't show every extreme that they name: `slot_image`: every image number appears in exactly one slot. band_start + band_len stays below 128.
All inputs are finite; a program needn't handle non-finite values.
Results may differ from the reference program's by a relative error of at most 0.0055.
Values may be sent and summed in bfloat16 or wider, within the bound.
A program may use at most 128 MiB of HBM per device.

```python
import math
import jax
import jax.numpy as jnp
from jax import lax

DW = 128
REFL = 8
FRAMES = 4
SWEEPS = 2
CELLS = 8192
ROWS = 128
ORIENTS = 32
IMAGES = 32


def place_ends(result, own_key, low, largest):
    place = [jax.random.randint(jax.random.fold_in(own_key, axis), (), 0, length) for axis, length in enumerate(result.shape)]
    longest = result.shape.index(max(result.shape))
    neighbour = place[:longest] + [(place[longest] + 1) % result.shape[longest]] + place[longest + 1:]
    return result.at[tuple(place)].set(low).at[tuple(neighbour)].set(largest)


def block_levels(stream_key, dims, pieces, least, largest):
    level, own = 1.0, jax.random.fold_in(stream_key, 6)
    for axis_at, shards_of in pieces:
        draws = jnp.exp(jax.random.uniform(jax.random.fold_in(own, axis_at), (shards_of,), jnp.float32, least / len(pieces), largest / len(pieces)))
        level = level * jnp.repeat(draws, dims[axis_at] // shards_of).reshape([-1 if axis == axis_at else 1 for axis in range(len(dims))])
    return level


def gaussian(stream_key, extent, spread, most, split=(), kind=jnp.bfloat16):
    entries = spread * jax.random.normal(stream_key, extent, jnp.float32)
    if split:
        entries = entries * block_levels(stream_key, extent, split, -0.22, 0.18)
    return jnp.clip(entries, -most, most).astype(kind)


def setup_inputs(seed: int = 0) -> dict:
    streams_of = jax.random.split(jax.random.key(seed), 8)
    volume = jnp.clip(2.0 * jax.random.uniform(streams_of[0], (ORIENTS, ROWS, CELLS), jnp.float32) ** block_levels(streams_of[0], (ORIENTS, ROWS, CELLS), ((0, 32),), -0.2, 0.2), 0.0, 2.0).astype(jnp.bfloat16)
    rays = gaussian(streams_of[1], (CELLS, REFL, DW), (CELLS * ORIENTS // FRAMES) ** -0.5, 0.0234375)
    band_start = place_ends(jax.random.randint(streams_of[2], (REFL, ORIENTS), 0, DW // 2), jax.random.fold_in(streams_of[2], 1), 0, (DW // 2) - 1).astype(jnp.int32)
    band_len = place_ends(jax.random.randint(streams_of[3], (REFL, ORIENTS), DW // 4, DW // 2 + 1), jax.random.fold_in(streams_of[3], 1), DW // 4, (DW // 2 + 1) - 1).astype(jnp.int32)
    slot_image = jax.random.permutation(streams_of[4], IMAGES).astype(jnp.int32)
    measured = gaussian(streams_of[5], (IMAGES, ROWS, DW), 1.0, 6.0, ((0, 32),), jnp.float32)
    relax = jnp.clip(jnp.exp(math.log(1.0) - 1.3862944 * jax.random.uniform(streams_of[6], (ORIENTS,), jnp.float32) ** block_levels(streams_of[6], (ORIENTS,), ((0, 32),), -0.2, 0.2)), 0.25, 1.0)
    return dict(volume=volume, rays=rays, band_start=band_start, band_len=band_len, slot_image=slot_image, measured=measured, relax=relax)


huber_delta = 0.5
sweep_rate = 0.2

def smooth_pass(extended, first_row, total_rows):
    middle = extended[:, 1:-1]
    row_count = middle.shape[1]
    global_rows = first_row + 1 + jnp.arange(row_count, dtype=jnp.int32)
    has_above = (global_rows > 0)[None, :, None]
    has_below = (global_rows < total_rows - 1)[None, :, None]
    from_above = jnp.clip(middle - extended[:, :-2], -huber_delta, huber_delta)
    from_below = jnp.clip(middle - extended[:, 2:], -huber_delta, huber_delta)
    row_flux = jnp.where(has_above, from_above, 0.0) + jnp.where(has_below, from_below, 0.0)
    return middle - sweep_rate * row_flux

def band_masks(band_start, band_len, detector):
    columns = jnp.arange(detector, dtype=jnp.int32)
    inside = (columns >= band_start[:, :, None]) & (columns < (band_start + band_len)[:, :, None])
    return inside.astype(jnp.float32)

def reference(volume, rays, band_start, band_len, slot_image, measured, relax):
    flat_rays = rays.reshape(CELLS, REFL * DW)
    band_mask = band_masks(band_start, band_len, DW)
    orient_ids = jnp.arange(ORIENTS, dtype=jnp.int32)
    reflections = jnp.arange(REFL, dtype=jnp.int32)
    frame_of = (orient_ids[:, None] + reflections[None, :]) % FRAMES
    frame_pick = (frame_of[:, :, None] == jnp.arange(FRAMES, dtype=jnp.int32)).astype(jnp.float32)

    def forward(total, orient_id):
        projected = jnp.dot(volume[orient_id], flat_rays, preferred_element_type=jnp.float32)
        projected = projected.reshape(ROWS, REFL, DW)
        term = jnp.einsum('kf,kd,rkd->kfrd', frame_pick[orient_id], band_mask[:, orient_id], projected)
        return (total + term, None)
    evolved = lax.scan(forward, jnp.zeros((REFL, FRAMES, ROWS, DW), jnp.float32), orient_ids)[0]
    evolved = evolved.reshape(IMAGES, ROWS, DW)
    residual = measured - evolved[slot_image]
    residual_sent = residual.astype(jnp.bfloat16)
    inverse = jnp.zeros((IMAGES,), jnp.int32).at[slot_image].set(jnp.arange(IMAGES, dtype=jnp.int32))
    by_image = residual_sent[inverse].reshape(REFL, FRAMES, ROWS, DW)
    step_gain = math.sqrt(CELLS * ORIENTS / (FRAMES * REFL * DW))
    rays_wide = rays.astype(jnp.float32)

    def backward(orient_id):
        picked = by_image[reflections, frame_of[orient_id]]
        masked = picked * band_mask[:, orient_id][:, None, :].astype(jnp.bfloat16)
        gradient = jnp.einsum('krd,ckd->rc', masked.astype(jnp.float32), rays_wide)
        density = volume[orient_id].astype(jnp.float32) + relax[orient_id] * step_gain * gradient
        for repeat in range(SWEEPS):
            extended = jnp.pad(density[None], ((0, 0), (1, 1), (0, 0)))
            density = smooth_pass(extended, -1, ROWS)[0]
        return density.astype(jnp.bfloat16)
    updated = lax.map(backward, orient_ids)
    return (updated, residual)
```

```python
import math

import jax
import jax.numpy as jnp
from jax import lax
from jax.experimental import pallas as pl
from jax.experimental.pallas import tpu as pltpu
from jax.sharding import PartitionSpec as P

FRAMES = 4
SWEEPS = 2


huber_delta = 0.5
sweep_rate = 0.2


def extended_2(cells, sides, width):
    for axis, dim in sides:
        count = lax.axis_size(axis)
        ends = count - 1
        head = lax.slice_in_dim(cells, 0, width, axis=dim)
        tail = lax.slice_in_dim(cells, cells.shape[dim] - width, cells.shape[dim], axis=dim)
        cells = jnp.concatenate(
            [
                lax.ppermute(tail, axis, [(i, (i + 1) % count) for i in range(ends)]),
                cells,
                lax.ppermute(head, axis, [((i + 1) % count, i) for i in range(ends)]),
            ],
            axis=dim,
        )
    return cells


def smooth_pass(extended, first_row, total_rows):
    middle = extended[:, 1:-1]
    row_count = middle.shape[1]
    global_rows = first_row + 1 + jnp.arange(row_count, dtype=jnp.int32)
    has_above = (global_rows > 0)[None, :, None]
    has_below = (global_rows < total_rows - 1)[None, :, None]
    from_above = jnp.clip(middle - extended[:, :-2], -huber_delta, huber_delta)
    from_below = jnp.clip(middle - extended[:, 2:], -huber_delta, huber_delta)
    row_flux = jnp.where(has_above, from_above, 0.0) + jnp.where(has_below, from_below, 0.0)
    return middle - sweep_rate * row_flux


def local(volume, rays, band_start, band_len, slot_image, measured, relax):
    or_dev, row_dev, cell_count = volume.shape
    reflections_n, detector = (rays.shape[1], rays.shape[2])
    images_n = reflections_n * FRAMES
    orient_groups = lax.axis_size("orient")
    orients_all = or_dev * orient_groups
    reflections = jnp.arange(reflections_n, dtype=jnp.int32)
    columns = jnp.arange(detector, dtype=jnp.int32)
    inside = (columns >= band_start[:, :, None]) & (columns < (band_start + band_len)[:, :, None])
    band_mask = inside.astype(jnp.float32)
    inverse = (
        jnp.zeros((images_n,), jnp.int32).at[slot_image].set(jnp.arange(images_n, dtype=jnp.int32))
    )
    flat_rays = rays.reshape(cell_count, reflections_n * detector)
    projected = jnp.dot(
        volume.reshape(or_dev * row_dev, cell_count), flat_rays, preferred_element_type=jnp.float32
    )
    projected = projected.reshape(or_dev, row_dev, reflections_n, detector)
    pixels = row_dev * detector
    contrib = jnp.einsum("kod,orkd->okrd", band_mask, projected).reshape(
        or_dev, reflections_n, pixels
    )
    parts = lax.all_to_all(contrib, "orient", split_axis=2, concat_axis=0, tiled=True)
    every_orient = jnp.arange(orients_all, dtype=jnp.int32)
    frame_all = (every_orient[:, None] + reflections[None, :]) % FRAMES
    pick_all = (frame_all[:, :, None] == jnp.arange(FRAMES, dtype=jnp.int32)).astype(jnp.float32)
    summed = jnp.einsum("okf,okp->kfp", pick_all, parts).reshape(images_n, parts.shape[2])
    owned = lax.all_to_all(summed[slot_image], "orient", split_axis=0, concat_axis=1, tiled=True)
    residual = measured - owned.reshape(measured.shape)
    sent = residual.astype(jnp.bfloat16).reshape(measured.shape[0], pixels)
    shares = lax.all_to_all(sent, "orient", split_axis=1, concat_axis=0, tiled=True)
    share_image = shares[inverse]
    selected = share_image[reflections[None, :] * FRAMES + frame_all]
    mine = lax.all_to_all(selected, "orient", split_axis=0, concat_axis=2, tiled=True)
    picked = mine.reshape(or_dev, reflections_n, row_dev, detector)
    masked = picked * jnp.transpose(band_mask, (1, 0, 2))[:, :, None, :].astype(jnp.bfloat16)
    gradient = jnp.einsum("okrd,ckd->orc", masked, rays, preferred_element_type=jnp.float32)
    step_gain = math.sqrt(cell_count * orients_all / (FRAMES * reflections_n * detector))
    density = volume.astype(jnp.float32) + relax[:, None, None] * step_gain * gradient
    total_rows = row_dev * lax.axis_size("slab")
    base_row = lax.axis_index("slab") * row_dev
    for repeat in range(SWEEPS):
        extended = extended_2(density, (("slab", 1),), 1)
        density = smooth_pass(extended, base_row - 1, total_rows)
    return (density.astype(jnp.bfloat16), residual)


def band(start_ref, len_ref, k, shape):
    column = lax.broadcasted_iota(jnp.int32, shape, len(shape) - 1)
    first = start_ref[k, 0]
    return (column >= first) & (column < first + len_ref[k, 0])


def forward_kernel(start_ref, len_ref, volume_ref, rays_ref, flat_ref, contrib_ref, wide, total):
    step = pl.program_id(0)
    cells, reflections_n, detector = rays_ref.shape
    members, _, share, _ = contrib_ref.shape

    @pl.when(step == 0)
    def _():
        total[...] = jnp.zeros_like(total)

    wide[...] = rays_ref[...].astype(jnp.float32).reshape(cells * reflections_n, detector)
    for k in range(reflections_n):
        part = wide[pl.ds(k, cells, stride=reflections_n), :]
        flat_ref[:, k * detector:(k + 1) * detector] = part.astype(jnp.bfloat16)
    total[...] += jnp.dot(volume_ref[...], flat_ref[...], preferred_element_type=jnp.float32)

    @pl.when(step == pl.num_programs(0) - 1)
    def _():
        for k in range(reflections_n):
            inside = band(start_ref, len_ref, k, (share, detector))
            for i in range(members):
                block = total[i * share:(i + 1) * share, k * detector:(k + 1) * detector]
                contrib_ref[i, k] = jnp.where(inside, block, 0.0).astype(jnp.bfloat16)


def exchange_kernel(
    n, start_ref, len_ref, slot_ref, inverse_ref, contrib_ref, measured_ref, masked_ref, residual_ref,
    pieces, images, gathered, outgoing, incoming,
    image_send, image_recv, piece_send, piece_recv, gather_send, gather_recv, quad_send, quad_recv,
):
    members, reflections_n, share, detector = contrib_ref.shape
    me = lax.axis_index("orient")
    group = lax.rem(me, FRAMES)
    member = me // FRAMES

    def remote(source, target, send, recv, device):
        return pltpu.make_async_remote_copy(
            src_ref=source, dst_ref=target, send_sem=send, recv_sem=recv,
            device_id={"orient": device}, device_id_type=pl.DeviceIdType.MESH,
        )

    barrier = pltpu.get_barrier_semaphore()

    @pl.loop(1, n)
    def _(s):
        pl.semaphore_signal(
            barrier, inc=1, device_id={"orient": lax.rem(me + s, n)},
            device_id_type=pl.DeviceIdType.MESH,
        )

    pl.semaphore_wait(barrier, n - 1)

    def piece_copy(s):
        other = lax.rem(member + s, members)
        return remote(
            contrib_ref.at[other], pieces.at[s - 1], piece_send.at[s - 1], piece_recv.at[s - 1],
            other * FRAMES + group,
        )

    def image_copy(s):
        device = lax.rem(me + s, n)
        return remote(
            measured_ref.at[device // FRAMES], images.at[s], image_send.at[s], image_recv.at[s], device
        )

    for s in range(1, members):
        piece_copy(s).start()

    @pl.loop(1, n)
    def _(s):
        image_copy(s).start()

    images[0] = measured_ref[member]
    total = contrib_ref[member].astype(jnp.float32)
    for s in range(1, members):
        piece_copy(s).wait()
        total = total + pieces[s - 1].astype(jnp.float32)

    @pl.loop(1, n)
    def _(s):
        image_copy(s).wait()

    for k in range(reflections_n):
        slot = inverse_ref[k * FRAMES + lax.rem(group + k, FRAMES)]
        seen = images[lax.rem(me - slot + n, n)].astype(jnp.float32)
        gathered[0, k] = (seen - total[k]).astype(jnp.bfloat16)

    def gather_copy(s):
        other = lax.rem(member + s, members)
        return remote(
            gathered.at[0], gathered.at[s], gather_send.at[s - 1], gather_recv.at[s - 1],
            other * FRAMES + group,
        )

    for s in range(1, members):
        gather_copy(s).start()
    for s in range(1, members):
        gather_copy(s).wait()

    def quad_copy(s):
        other = lax.rem(group + s, FRAMES)
        return remote(
            outgoing.at[s - 1], incoming.at[s], quad_send.at[s - 1], quad_recv.at[s - 1],
            member * FRAMES + other,
        )

    for s in range(FRAMES):
        wanted = slot_ref[member * FRAMES + lax.rem(group + s, FRAMES)] // FRAMES
        for i in range(members):
            block = gathered[i, wanted]
            if s == 0:
                incoming[0, i] = block
            else:
                outgoing[s - 1, i] = block
        if s:
            quad_copy(s).start()
    for k in range(reflections_n):
        inside = band(start_ref, len_ref, k, (share, detector))
        for i in range(members):
            owner = lax.rem(member - i + members, members)
            rows = pl.ds(pl.multiple_of(owner * share, share), share)
            masked_ref[rows, k * detector:(k + 1) * detector] = jnp.where(
                inside, gathered[i, k].astype(jnp.float32), 0.0
            ).astype(jnp.bfloat16)
    for s in range(1, FRAMES):
        quad_copy(s).wait()
    mine = slot_ref[me]
    held = lax.rem(lax.rem(mine, FRAMES) - lax.rem(mine // FRAMES, FRAMES) + FRAMES, FRAMES)
    back = lax.rem(group - held + FRAMES, FRAMES)
    for i in range(members):
        owner = lax.rem(member - i + members, members)
        rows = pl.ds(pl.multiple_of(owner * share, share), share)
        residual_ref[rows, :] = incoming[back, i].astype(jnp.float32)


def backward_kernel(scale_ref, volume_ref, flat_ref, masked_ref, updated_ref):
    gradient = lax.dot_general(
        masked_ref[...], flat_ref[...], (((1,), (1,)), ((), ())), preferred_element_type=jnp.float32
    )
    density = volume_ref[...].astype(jnp.float32) + scale_ref[0] * gradient
    edge = jnp.zeros_like(density[:1])
    for repeat in range(SWEEPS):
        flux = jnp.clip(density[1:] - density[:-1], -huber_delta, huber_delta)
        above = jnp.concatenate([edge, flux], axis=0)
        below = jnp.concatenate([flux, edge], axis=0)
        density = density - sweep_rate * (above - below)
    updated_ref[...] = density.astype(jnp.bfloat16)


def fast(volume, rays, band_start, band_len, slot_image, measured, relax):
    _, rows, cell_count = volume.shape
    _, reflections_n, detector = rays.shape
    n = lax.axis_size("orient")
    members = n // FRAMES
    share = rows // members
    images_n = slot_image.shape[0]
    wide_n = reflections_n * detector
    tile = min(512, cell_count)
    volume = volume.reshape(rows, cell_count)
    smem = pl.BlockSpec(memory_space=pltpu.SMEM)
    vmem = pl.BlockSpec(memory_space=pltpu.VMEM)
    flat, contrib = pl.pallas_call(
        forward_kernel,
        grid=(cell_count // tile,),
        in_specs=[
            smem,
            smem,
            pl.BlockSpec((rows, tile), lambda c: (0, c)),
            pl.BlockSpec((tile, reflections_n, detector), lambda c: (c, 0, 0)),
        ],
        out_specs=[
            pl.BlockSpec((tile, wide_n), lambda c: (c, 0)),
            pl.BlockSpec((members, reflections_n, share, detector), lambda c: (0, 0, 0, 0)),
        ],
        out_shape=[
            jax.ShapeDtypeStruct((cell_count, wide_n), jnp.bfloat16),
            jax.ShapeDtypeStruct((members, reflections_n, share, detector), jnp.bfloat16),
        ],
        scratch_shapes=[
            pltpu.VMEM((tile * reflections_n, detector), jnp.float32),
            pltpu.VMEM((rows, wide_n), jnp.float32),
        ],
        compiler_params=pltpu.CompilerParams(vmem_limit_bytes=32 * 2**20),
        name="forward",
    )(band_start, band_len, volume, rays)
    inverse = jnp.sum(
        jnp.where(
            slot_image[None, :] == jnp.arange(images_n, dtype=jnp.int32)[:, None],
            jnp.arange(images_n, dtype=jnp.int32)[None, :],
            0,
        ),
        axis=1,
    )
    narrow = measured.astype(jnp.bfloat16).reshape(members, share, detector)
    block = (reflections_n, share, detector)
    masked, residual = pl.pallas_call(
        lambda *refs: exchange_kernel(n, *refs),
        in_specs=[smem, smem, smem, smem, vmem, vmem],
        out_specs=[vmem, vmem],
        out_shape=[
            jax.ShapeDtypeStruct((rows, wide_n), jnp.bfloat16),
            jax.ShapeDtypeStruct((rows, detector), jnp.float32),
        ],
        scratch_shapes=[
            pltpu.VMEM((members - 1,) + block, jnp.bfloat16),
            pltpu.VMEM((n, share, detector), jnp.bfloat16),
            pltpu.VMEM((members,) + block, jnp.bfloat16),
            pltpu.VMEM((FRAMES - 1, members, share, detector), jnp.bfloat16),
            pltpu.VMEM((FRAMES, members, share, detector), jnp.bfloat16),
            pltpu.SemaphoreType.DMA((n,)),
            pltpu.SemaphoreType.DMA((n,)),
            pltpu.SemaphoreType.DMA((members - 1,)),
            pltpu.SemaphoreType.DMA((members - 1,)),
            pltpu.SemaphoreType.DMA((members - 1,)),
            pltpu.SemaphoreType.DMA((members - 1,)),
            pltpu.SemaphoreType.DMA((FRAMES - 1,)),
            pltpu.SemaphoreType.DMA((FRAMES - 1,)),
        ],
        compiler_params=pltpu.CompilerParams(
            collective_id=0, has_side_effects=True, vmem_limit_bytes=16 * 2**20
        ),
        name="exchange",
    )(band_start, band_len, slot_image, inverse, contrib, narrow)
    step_gain = math.sqrt(cell_count * n / (FRAMES * reflections_n * detector))
    updated = pl.pallas_call(
        backward_kernel,
        grid=(cell_count // tile,),
        in_specs=[
            smem,
            pl.BlockSpec((rows, tile), lambda c: (0, c)),
            pl.BlockSpec((tile, wide_n), lambda c: (c, 0)),
            pl.BlockSpec((rows, wide_n), lambda c: (0, 0)),
        ],
        out_specs=pl.BlockSpec((rows, tile), lambda c: (0, c)),
        out_shape=jax.ShapeDtypeStruct((rows, cell_count), jnp.bfloat16),
        compiler_params=pltpu.CompilerParams(vmem_limit_bytes=32 * 2**20),
        name="backward",
    )(relax * step_gain, volume, flat, masked)
    return updated[None], residual[None]


def chosen(*operands):
    volume, rays, _, _, slot_image, measured, _ = operands
    n = lax.axis_size("orient")
    plain = (
        lax.axis_size("slab") == 1
        and volume.shape[0] == 1
        and measured.shape[0] == 1
        and n % FRAMES == 0
        and n > FRAMES
        and volume.shape[1] % (16 * (n // FRAMES)) == 0
        and volume.shape[2] % min(512, volume.shape[2]) == 0
        and rays.shape[1] % 8 == 0
        and rays.shape[2] % 128 == 0
    )
    return fast(*operands) if plain else local(*operands)


def solution(mesh):
    placed = (
        P("orient", "slab", None),
        P(),
        P(None, "orient"),
        P(None, "orient"),
        P(),
        P("orient", "slab", None),
        P("orient"),
    )
    return jax.shard_map(
        chosen,
        mesh=mesh,
        in_specs=placed,
        out_specs=(P("orient", "slab", None), P("orient", "slab", None)),
        check_vma=False,
    )
```

```python
import functools
import math

import jax
import jax.numpy as jnp
from jax import lax
from jax.experimental import pallas as pl
from jax.experimental.pallas import tpu as pltpu
from jax.sharding import PartitionSpec as P

FRAMES = 4
SWEEPS = 2


huber_delta = 0.5
sweep_rate = 0.2


def extended_2(cells, sides, width):
    for axis, dim in sides:
        count = lax.axis_size(axis)
        ends = count - 1
        head = lax.slice_in_dim(cells, 0, width, axis=dim)
        tail = lax.slice_in_dim(cells, cells.shape[dim] - width, cells.shape[dim], axis=dim)
        cells = jnp.concatenate(
            [
                lax.ppermute(tail, axis, [(i, (i + 1) % count) for i in range(ends)]),
                cells,
                lax.ppermute(head, axis, [((i + 1) % count, i) for i in range(ends)]),
            ],
            axis=dim,
        )
    return cells


def smooth_pass(extended, first_row, total_rows):
    middle = extended[:, 1:-1]
    row_count = middle.shape[1]
    global_rows = first_row + 1 + jnp.arange(row_count, dtype=jnp.int32)
    has_above = (global_rows > 0)[None, :, None]
    has_below = (global_rows < total_rows - 1)[None, :, None]
    from_above = jnp.clip(middle - extended[:, :-2], -huber_delta, huber_delta)
    from_below = jnp.clip(middle - extended[:, 2:], -huber_delta, huber_delta)
    row_flux = jnp.where(has_above, from_above, 0.0) + jnp.where(has_below, from_below, 0.0)
    return middle - sweep_rate * row_flux


def local(volume, rays, band_start, band_len, slot_image, measured, relax):
    or_dev, row_dev, cell_count = volume.shape
    reflections_n, detector = (rays.shape[1], rays.shape[2])
    images_n = reflections_n * FRAMES
    orient_groups = lax.axis_size("orient")
    orients_all = or_dev * orient_groups
    reflections = jnp.arange(reflections_n, dtype=jnp.int32)
    columns = jnp.arange(detector, dtype=jnp.int32)
    inside = (columns >= band_start[:, :, None]) & (columns < (band_start + band_len)[:, :, None])
    band_mask = inside.astype(jnp.float32)
    inverse = (
        jnp.zeros((images_n,), jnp.int32).at[slot_image].set(jnp.arange(images_n, dtype=jnp.int32))
    )
    flat_rays = rays.reshape(cell_count, reflections_n * detector)
    projected = jnp.dot(
        volume.reshape(or_dev * row_dev, cell_count), flat_rays, preferred_element_type=jnp.float32
    )
    projected = projected.reshape(or_dev, row_dev, reflections_n, detector)
    pixels = row_dev * detector
    contrib = jnp.einsum("kod,orkd->okrd", band_mask, projected).reshape(
        or_dev, reflections_n, pixels
    )
    parts = lax.all_to_all(contrib, "orient", split_axis=2, concat_axis=0, tiled=True)
    every_orient = jnp.arange(orients_all, dtype=jnp.int32)
    frame_all = (every_orient[:, None] + reflections[None, :]) % FRAMES
    pick_all = (frame_all[:, :, None] == jnp.arange(FRAMES, dtype=jnp.int32)).astype(jnp.float32)
    summed = jnp.einsum("okf,okp->kfp", pick_all, parts).reshape(images_n, parts.shape[2])
    owned = lax.all_to_all(summed[slot_image], "orient", split_axis=0, concat_axis=1, tiled=True)
    residual = measured - owned.reshape(measured.shape)
    sent = residual.astype(jnp.bfloat16).reshape(measured.shape[0], pixels)
    shares = lax.all_to_all(sent, "orient", split_axis=1, concat_axis=0, tiled=True)
    share_image = shares[inverse]
    selected = share_image[reflections[None, :] * FRAMES + frame_all]
    mine = lax.all_to_all(selected, "orient", split_axis=0, concat_axis=2, tiled=True)
    picked = mine.reshape(or_dev, reflections_n, row_dev, detector)
    masked = picked * jnp.transpose(band_mask, (1, 0, 2))[:, :, None, :].astype(jnp.bfloat16)
    gradient = jnp.einsum("okrd,ckd->orc", masked, rays, preferred_element_type=jnp.float32)
    step_gain = math.sqrt(cell_count * orients_all / (FRAMES * reflections_n * detector))
    density = volume.astype(jnp.float32) + relax[:, None, None] * step_gain * gradient
    total_rows = row_dev * lax.axis_size("slab")
    base_row = lax.axis_index("slab") * row_dev
    for repeat in range(SWEEPS):
        extended = extended_2(density, (("slab", 1),), 1)
        density = smooth_pass(extended, base_row - 1, total_rows)
    return (density.astype(jnp.bfloat16), residual)


def band(start_ref, len_ref, k, shape):
    column = lax.broadcasted_iota(jnp.int32, shape, len(shape) - 1)
    first = start_ref[k, 0]
    return (column >= first) & (column < first + len_ref[k, 0])


def forward_kernel(start_ref, len_ref, volume_ref, rays_ref, flat_ref, contrib_ref, wide, total):
    step = pl.program_id(0)
    cells, reflections_n, detector = rays_ref.shape
    members, _, share, _ = contrib_ref.shape

    @pl.when(step == 0)
    def _():
        total[...] = jnp.zeros_like(total)

    wide[...] = rays_ref[...].astype(jnp.float32).reshape(cells * reflections_n, detector)
    for k in range(reflections_n):
        part = wide[pl.ds(k, cells, stride=reflections_n), :]
        flat_ref[:, k * detector:(k + 1) * detector] = part.astype(jnp.bfloat16)
    total[...] += jnp.dot(volume_ref[...], flat_ref[...], preferred_element_type=jnp.float32)

    @pl.when(step == pl.num_programs(0) - 1)
    def _():
        for k in range(reflections_n):
            inside = band(start_ref, len_ref, k, (share, detector))
            for i in range(members):
                block = total[i * share:(i + 1) * share, k * detector:(k + 1) * detector]
                contrib_ref[i, k] = jnp.where(inside, block, 0.0).astype(jnp.bfloat16)


def exchange_kernel(
    n, start_ref, len_ref, slot_ref, contrib_ref, measured_ref, masked_ref, residual_ref,
    narrow, pieces, images, gathered, outgoing, incoming,
    image_send, image_recv, piece_send, piece_recv, gather_send, gather_recv, quad_send, quad_recv,
):
    members, reflections_n, share, detector = contrib_ref.shape
    me = lax.axis_index("orient")
    group = lax.rem(me, FRAMES)
    member = me // FRAMES

    def remote(source, target, send, recv, device):
        return pltpu.make_async_remote_copy(
            src_ref=source, dst_ref=target, send_sem=send, recv_sem=recv,
            device_id={"orient": device}, device_id_type=pl.DeviceIdType.MESH,
        )

    barrier = pltpu.get_barrier_semaphore()

    @pl.loop(1, n)
    def _(s):
        pl.semaphore_signal(
            barrier, inc=1, device_id={"orient": lax.rem(me + s, n)},
            device_id_type=pl.DeviceIdType.MESH,
        )

    narrow[...] = measured_ref[...].astype(jnp.bfloat16)
    pl.semaphore_wait(barrier, n - 1)

    def piece_copy(s):
        other = lax.rem(member + s, members)
        return remote(
            contrib_ref.at[other], pieces.at[s - 1], piece_send.at[s - 1], piece_recv.at[s - 1],
            other * FRAMES + group,
        )

    def image_copy(s):
        device = lax.rem(me + s, n)
        return remote(
            narrow.at[device // FRAMES], images.at[s], image_send.at[s], image_recv.at[s], device
        )

    for s in range(1, members):
        piece_copy(s).start()

    @pl.loop(1, n)
    def _(s):
        image_copy(s).start()

    images[0] = narrow[member]
    total = contrib_ref[member].astype(jnp.float32)
    for s in range(1, members):
        piece_copy(s).wait()
        total = total + pieces[s - 1].astype(jnp.float32)

    @pl.loop(1, n)
    def _(s):
        image_copy(s).wait()

    for k in range(reflections_n):
        image = k * FRAMES + lax.rem(group + k, FRAMES)
        slot = jnp.int32(0)
        for j in range(slot_ref.shape[0]):
            slot = jnp.where(slot_ref[j] == image, j, slot)
        seen = images[lax.rem(me - slot + n, n)].astype(jnp.float32)
        gathered[0, k] = (seen - total[k]).astype(jnp.bfloat16)

    def gather_copy(s):
        other = lax.rem(member + s, members)
        return remote(
            gathered.at[0], gathered.at[s], gather_send.at[s - 1], gather_recv.at[s - 1],
            other * FRAMES + group,
        )

    for s in range(1, members):
        gather_copy(s).start()
    for s in range(1, members):
        gather_copy(s).wait()

    def quad_copy(s):
        other = lax.rem(group + s, FRAMES)
        return remote(
            outgoing.at[s - 1], incoming.at[s], quad_send.at[s - 1], quad_recv.at[s - 1],
            member * FRAMES + other,
        )

    for s in range(FRAMES):
        wanted = slot_ref[member * FRAMES + lax.rem(group + s, FRAMES)] // FRAMES
        for i in range(members):
            block = gathered[i, wanted]
            if s == 0:
                incoming[0, i] = block
            else:
                outgoing[s - 1, i] = block
        if s:
            quad_copy(s).start()
    for k in range(reflections_n):
        inside = band(start_ref, len_ref, k, (share, detector))
        for i in range(members):
            owner = lax.rem(member - i + members, members)
            rows = pl.ds(pl.multiple_of(owner * share, share), share)
            masked_ref[rows, k * detector:(k + 1) * detector] = jnp.where(
                inside, gathered[i, k].astype(jnp.float32), 0.0
            ).astype(jnp.bfloat16)
    for s in range(1, FRAMES):
        quad_copy(s).wait()
    mine = slot_ref[me]
    held = lax.rem(lax.rem(mine, FRAMES) - lax.rem(mine // FRAMES, FRAMES) + FRAMES, FRAMES)
    back = lax.rem(group - held + FRAMES, FRAMES)
    for i in range(members):
        owner = lax.rem(member - i + members, members)
        rows = pl.ds(pl.multiple_of(owner * share, share), share)
        residual_ref[rows, :] = incoming[back, i].astype(jnp.float32)


def backward_kernel(step_gain, relax_ref, volume_ref, flat_ref, masked_ref, updated_ref):
    gradient = lax.dot_general(
        masked_ref[...], flat_ref[...], (((1,), (1,)), ((), ())), preferred_element_type=jnp.float32
    )
    density = volume_ref[...].astype(jnp.float32) + relax_ref[0] * step_gain * gradient
    edge = jnp.zeros_like(density[:1])
    for repeat in range(SWEEPS):
        flux = jnp.clip(density[1:] - density[:-1], -huber_delta, huber_delta)
        above = jnp.concatenate([edge, flux], axis=0)
        below = jnp.concatenate([flux, edge], axis=0)
        density = density - sweep_rate * (above - below)
    updated_ref[...] = density.astype(jnp.bfloat16)


def fast(volume, rays, band_start, band_len, slot_image, measured, relax):
    _, rows, cell_count = volume.shape
    _, reflections_n, detector = rays.shape
    n = lax.axis_size("orient")
    members = n // FRAMES
    share = rows // members
    images_n = slot_image.shape[0]
    wide_n = reflections_n * detector
    tile = min(512, cell_count)
    volume = volume.reshape(rows, cell_count)
    smem = pl.BlockSpec(memory_space=pltpu.SMEM)
    vmem = pl.BlockSpec(memory_space=pltpu.VMEM)
    flat, contrib = pl.pallas_call(
        forward_kernel,
        grid=(cell_count // tile,),
        in_specs=[
            smem,
            smem,
            pl.BlockSpec((rows, tile), lambda c: (0, c)),
            pl.BlockSpec((tile, reflections_n, detector), lambda c: (c, 0, 0)),
        ],
        out_specs=[
            pl.BlockSpec((tile, wide_n), lambda c: (c, 0)),
            pl.BlockSpec((members, reflections_n, share, detector), lambda c: (0, 0, 0, 0)),
        ],
        out_shape=[
            jax.ShapeDtypeStruct((cell_count, wide_n), jnp.bfloat16),
            jax.ShapeDtypeStruct((members, reflections_n, share, detector), jnp.bfloat16),
        ],
        scratch_shapes=[
            pltpu.VMEM((tile * reflections_n, detector), jnp.float32),
            pltpu.VMEM((rows, wide_n), jnp.float32),
        ],
        compiler_params=pltpu.CompilerParams(vmem_limit_bytes=60 * 2**20),
        name="forward",
    )(band_start, band_len, volume, rays)
    block = (reflections_n, share, detector)
    masked, residual = pl.pallas_call(
        lambda *refs: exchange_kernel(n, *refs),
        in_specs=[smem, smem, smem, vmem, vmem],
        out_specs=[vmem, vmem],
        out_shape=[
            jax.ShapeDtypeStruct((rows, wide_n), jnp.bfloat16),
            jax.ShapeDtypeStruct((rows, detector), jnp.float32),
        ],
        scratch_shapes=[
            pltpu.VMEM((members, share, detector), jnp.bfloat16),
            pltpu.VMEM((members - 1,) + block, jnp.bfloat16),
            pltpu.VMEM((n, share, detector), jnp.bfloat16),
            pltpu.VMEM((members,) + block, jnp.bfloat16),
            pltpu.VMEM((FRAMES - 1, members, share, detector), jnp.bfloat16),
            pltpu.VMEM((FRAMES, members, share, detector), jnp.bfloat16),
            pltpu.SemaphoreType.DMA((n,)),
            pltpu.SemaphoreType.DMA((n,)),
            pltpu.SemaphoreType.DMA((members - 1,)),
            pltpu.SemaphoreType.DMA((members - 1,)),
            pltpu.SemaphoreType.DMA((members - 1,)),
            pltpu.SemaphoreType.DMA((members - 1,)),
            pltpu.SemaphoreType.DMA((FRAMES - 1,)),
            pltpu.SemaphoreType.DMA((FRAMES - 1,)),
        ],
        compiler_params=pltpu.CompilerParams(
            collective_id=0, has_side_effects=True, vmem_limit_bytes=60 * 2**20
        ),
        name="exchange",
    )(band_start, band_len, slot_image, contrib, measured.reshape(members, share, detector))
    step_gain = math.sqrt(cell_count * n / (FRAMES * reflections_n * detector))
    updated = pl.pallas_call(
        functools.partial(backward_kernel, step_gain),
        grid=(cell_count // tile,),
        in_specs=[
            smem,
            pl.BlockSpec((rows, tile), lambda c: (0, c)),
            pl.BlockSpec((tile, wide_n), lambda c: (c, 0)),
            pl.BlockSpec((rows, wide_n), lambda c: (0, 0)),
        ],
        out_specs=pl.BlockSpec((rows, tile), lambda c: (0, c)),
        out_shape=jax.ShapeDtypeStruct((rows, cell_count), jnp.bfloat16),
        compiler_params=pltpu.CompilerParams(vmem_limit_bytes=60 * 2**20),
        name="backward",
    )(relax, volume, flat, masked)
    return updated[None], residual[None]


def chosen(*operands):
    volume, rays, _, _, slot_image, measured, _ = operands
    n = lax.axis_size("orient")
    plain = (
        lax.axis_size("slab") == 1
        and volume.shape[0] == 1
        and measured.shape[0] == 1
        and n % FRAMES == 0
        and n > FRAMES
        and volume.shape[1] % (16 * (n // FRAMES)) == 0
        and volume.shape[2] % min(512, volume.shape[2]) == 0
        and rays.shape[1] % 8 == 0
        and rays.shape[2] % 128 == 0
    )
    return fast(*operands) if plain else local(*operands)


def solution(mesh):
    placed = (
        P("orient", "slab", None),
        P(),
        P(None, "orient"),
        P(None, "orient"),
        P(),
        P("orient", "slab", None),
        P("orient"),
    )
    return jax.shard_map(
        chosen,
        mesh=mesh,
        in_specs=placed,
        out_specs=(P("orient", "slab", None), P("orient", "slab", None)),
        check_vma=False,
    )
```

```python
import functools
import math

import jax
import jax.numpy as jnp
from jax import lax
from jax.experimental import pallas as pl
from jax.experimental.pallas import tpu as pltpu
from jax.sharding import PartitionSpec as P

FRAMES = 4
SWEEPS = 2


huber_delta = 0.5
sweep_rate = 0.2


def extended_2(cells, sides, width):
    for axis, dim in sides:
        count = lax.axis_size(axis)
        ends = count - 1
        head = lax.slice_in_dim(cells, 0, width, axis=dim)
        tail = lax.slice_in_dim(cells, cells.shape[dim] - width, cells.shape[dim], axis=dim)
        cells = jnp.concatenate(
            [
                lax.ppermute(tail, axis, [(i, (i + 1) % count) for i in range(ends)]),
                cells,
                lax.ppermute(head, axis, [((i + 1) % count, i) for i in range(ends)]),
            ],
            axis=dim,
        )
    return cells


def smooth_pass(extended, first_row, total_rows):
    middle = extended[:, 1:-1]
    row_count = middle.shape[1]
    global_rows = first_row + 1 + jnp.arange(row_count, dtype=jnp.int32)
    has_above = (global_rows > 0)[None, :, None]
    has_below = (global_rows < total_rows - 1)[None, :, None]
    from_above = jnp.clip(middle - extended[:, :-2], -huber_delta, huber_delta)
    from_below = jnp.clip(middle - extended[:, 2:], -huber_delta, huber_delta)
    row_flux = jnp.where(has_above, from_above, 0.0) + jnp.where(has_below, from_below, 0.0)
    return middle - sweep_rate * row_flux


def local(volume, rays, band_start, band_len, slot_image, measured, relax):
    or_dev, row_dev, cell_count = volume.shape
    reflections_n, detector = (rays.shape[1], rays.shape[2])
    images_n = reflections_n * FRAMES
    orient_groups = lax.axis_size("orient")
    orients_all = or_dev * orient_groups
    reflections = jnp.arange(reflections_n, dtype=jnp.int32)
    columns = jnp.arange(detector, dtype=jnp.int32)
    inside = (columns >= band_start[:, :, None]) & (columns < (band_start + band_len)[:, :, None])
    band_mask = inside.astype(jnp.float32)
    inverse = (
        jnp.zeros((images_n,), jnp.int32).at[slot_image].set(jnp.arange(images_n, dtype=jnp.int32))
    )
    flat_rays = rays.reshape(cell_count, reflections_n * detector)
    projected = jnp.dot(
        volume.reshape(or_dev * row_dev, cell_count), flat_rays, preferred_element_type=jnp.float32
    )
    projected = projected.reshape(or_dev, row_dev, reflections_n, detector)
    pixels = row_dev * detector
    contrib = jnp.einsum("kod,orkd->okrd", band_mask, projected).reshape(
        or_dev, reflections_n, pixels
    )
    parts = lax.all_to_all(contrib, "orient", split_axis=2, concat_axis=0, tiled=True)
    every_orient = jnp.arange(orients_all, dtype=jnp.int32)
    frame_all = (every_orient[:, None] + reflections[None, :]) % FRAMES
    pick_all = (frame_all[:, :, None] == jnp.arange(FRAMES, dtype=jnp.int32)).astype(jnp.float32)
    summed = jnp.einsum("okf,okp->kfp", pick_all, parts).reshape(images_n, parts.shape[2])
    owned = lax.all_to_all(summed[slot_image], "orient", split_axis=0, concat_axis=1, tiled=True)
    residual = measured - owned.reshape(measured.shape)
    sent = residual.astype(jnp.bfloat16).reshape(measured.shape[0], pixels)
    shares = lax.all_to_all(sent, "orient", split_axis=1, concat_axis=0, tiled=True)
    share_image = shares[inverse]
    selected = share_image[reflections[None, :] * FRAMES + frame_all]
    mine = lax.all_to_all(selected, "orient", split_axis=0, concat_axis=2, tiled=True)
    picked = mine.reshape(or_dev, reflections_n, row_dev, detector)
    masked = picked * jnp.transpose(band_mask, (1, 0, 2))[:, :, None, :].astype(jnp.bfloat16)
    gradient = jnp.einsum("okrd,ckd->orc", masked, rays, preferred_element_type=jnp.float32)
    step_gain = math.sqrt(cell_count * orients_all / (FRAMES * reflections_n * detector))
    density = volume.astype(jnp.float32) + relax[:, None, None] * step_gain * gradient
    total_rows = row_dev * lax.axis_size("slab")
    base_row = lax.axis_index("slab") * row_dev
    for repeat in range(SWEEPS):
        extended = extended_2(density, (("slab", 1),), 1)
        density = smooth_pass(extended, base_row - 1, total_rows)
    return (density.astype(jnp.bfloat16), residual)


def band(start_ref, len_ref, k, shape):
    column = lax.broadcasted_iota(jnp.int32, shape, len(shape) - 1)
    first = start_ref[k, 0]
    return (column >= first) & (column < first + len_ref[k, 0])


def forward_kernel(start_ref, len_ref, volume_ref, rays_ref, flat_ref, contrib_ref, wide, total):
    step = pl.program_id(0)
    cells, reflections_n, detector = rays_ref.shape
    members, _, share, _ = contrib_ref.shape

    @pl.when(step == 0)
    def _():
        total[...] = jnp.zeros_like(total)

    wide[...] = rays_ref[...].astype(jnp.float32).reshape(cells * reflections_n, detector)
    for k in range(reflections_n):
        part = wide[pl.ds(k, cells, stride=reflections_n), :]
        flat_ref[:, k * detector:(k + 1) * detector] = part.astype(jnp.bfloat16)
    total[...] += jnp.dot(volume_ref[...], flat_ref[...], preferred_element_type=jnp.float32)

    @pl.when(step == pl.num_programs(0) - 1)
    def _():
        for k in range(reflections_n):
            inside = band(start_ref, len_ref, k, (share, detector))
            for i in range(members):
                block = total[i * share:(i + 1) * share, k * detector:(k + 1) * detector]
                contrib_ref[i, k] = jnp.where(inside, block, 0.0).astype(jnp.bfloat16)


def exchange_kernel(
    n, start_ref, len_ref, slot_ref, contrib_ref, measured_ref, masked_ref, residual_ref,
    narrow, pieces, images, gathered, outgoing, incoming,
    image_send, image_recv, piece_send, piece_recv, gather_send, gather_recv, quad_send, quad_recv,
):
    members, reflections_n, share, detector = contrib_ref.shape
    me = lax.axis_index("orient")
    group = lax.rem(me, FRAMES)
    member = me // FRAMES

    def remote(source, target, send, recv, device):
        return pltpu.make_async_remote_copy(
            src_ref=source, dst_ref=target, send_sem=send, recv_sem=recv,
            device_id={"orient": device}, device_id_type=pl.DeviceIdType.MESH,
        )

    barrier = pltpu.get_barrier_semaphore()

    @pl.loop(1, n)
    def _(s):
        pl.semaphore_signal(
            barrier, inc=1, device_id={"orient": lax.rem(me + s, n)},
            device_id_type=pl.DeviceIdType.MESH,
        )

    narrow[...] = measured_ref[...].astype(jnp.bfloat16)
    pl.semaphore_wait(barrier, n - 1)

    def piece_copy(s):
        other = lax.rem(member + s, members)
        return remote(
            contrib_ref.at[other], pieces.at[s - 1], piece_send.at[s - 1], piece_recv.at[s - 1],
            other * FRAMES + group,
        )

    def image_copy(s):
        device = lax.rem(me + s, n)
        return remote(
            narrow.at[device // FRAMES], images.at[s], image_send.at[s], image_recv.at[s], device
        )

    for s in range(1, members):
        piece_copy(s).start()

    @pl.loop(1, n)
    def _(s):
        image_copy(s).start()

    images[0] = narrow[member]
    total = contrib_ref[member].astype(jnp.float32)
    for s in range(1, members):
        piece_copy(s).wait()
        total = total + pieces[s - 1].astype(jnp.float32)

    @pl.loop(1, n)
    def _(s):
        image_copy(s).wait()

    for k in range(reflections_n):
        image = k * FRAMES + lax.rem(group + k, FRAMES)
        slot = jnp.int32(0)
        for j in range(slot_ref.shape[0]):
            slot = jnp.where(slot_ref[j] == image, j, slot)
        seen = images[lax.rem(me - slot + n, n)].astype(jnp.float32)
        gathered[0, k] = (seen - total[k]).astype(jnp.bfloat16)

    def gather_copy(s):
        other = lax.rem(member + s, members)
        return remote(
            gathered.at[0], gathered.at[s], gather_send.at[s - 1], gather_recv.at[s - 1],
            other * FRAMES + group,
        )

    for s in range(1, members):
        gather_copy(s).start()
    for s in range(1, members):
        gather_copy(s).wait()

    def quad_copy(s):
        other = lax.rem(group + s, FRAMES)
        return remote(
            outgoing.at[s - 1], incoming.at[s], quad_send.at[s - 1], quad_recv.at[s - 1],
            member * FRAMES + other,
        )

    for s in range(FRAMES):
        wanted = slot_ref[member * FRAMES + lax.rem(group + s, FRAMES)] // FRAMES
        for i in range(members):
            block = gathered[i, wanted]
            if s == 0:
                incoming[0, i] = block
            else:
                outgoing[s - 1, i] = block
        if s:
            quad_copy(s).start()
    for k in range(reflections_n):
        inside = band(start_ref, len_ref, k, (share, detector))
        for i in range(members):
            owner = lax.rem(member - i + members, members)
            rows = pl.ds(pl.multiple_of(owner * share, share), share)
            masked_ref[rows, k * detector:(k + 1) * detector] = jnp.where(
                inside, gathered[i, k].astype(jnp.float32), 0.0
            ).astype(jnp.bfloat16)
    for s in range(1, FRAMES):
        quad_copy(s).wait()
    mine = slot_ref[me]
    held = lax.rem(lax.rem(mine, FRAMES) - lax.rem(mine // FRAMES, FRAMES) + FRAMES, FRAMES)
    back = lax.rem(group - held + FRAMES, FRAMES)
    for i in range(members):
        owner = lax.rem(member - i + members, members)
        rows = pl.ds(pl.multiple_of(owner * share, share), share)
        residual_ref[rows, :] = incoming[back, i].astype(jnp.float32)


def backward_kernel(step_gain, relax_ref, volume_ref, flat_ref, masked_ref, updated_ref):
    gradient = lax.dot_general(
        masked_ref[...], flat_ref[...], (((1,), (1,)), ((), ())), preferred_element_type=jnp.float32
    )
    density = volume_ref[...].astype(jnp.float32) + relax_ref[0] * step_gain * gradient
    edge = jnp.zeros_like(density[:1])
    for repeat in range(SWEEPS):
        flux = jnp.clip(density[1:] - density[:-1], -huber_delta, huber_delta)
        above = jnp.concatenate([edge, flux], axis=0)
        below = jnp.concatenate([flux, edge], axis=0)
        density = density - sweep_rate * (above - below)
    updated_ref[...] = density.astype(jnp.bfloat16)


def fast(volume, rays, band_start, band_len, slot_image, measured, relax):
    _, rows, cell_count = volume.shape
    _, reflections_n, detector = rays.shape
    n = lax.axis_size("orient")
    members = n // FRAMES
    share = rows // members
    images_n = slot_image.shape[0]
    wide_n = reflections_n * detector
    tile = min(512, cell_count)
    volume = volume.reshape(rows, cell_count)
    smem = pl.BlockSpec(memory_space=pltpu.SMEM)
    vmem = pl.BlockSpec(memory_space=pltpu.VMEM)
    flat, contrib = pl.pallas_call(
        forward_kernel,
        grid=(cell_count // tile,),
        in_specs=[
            smem,
            smem,
            pl.BlockSpec((rows, tile), lambda c: (0, c)),
            pl.BlockSpec((tile, reflections_n, detector), lambda c: (c, 0, 0)),
        ],
        out_specs=[
            pl.BlockSpec((tile, wide_n), lambda c: (c, 0)),
            pl.BlockSpec((members, reflections_n, share, detector), lambda c: (0, 0, 0, 0)),
        ],
        out_shape=[
            jax.ShapeDtypeStruct((cell_count, wide_n), jnp.bfloat16),
            jax.ShapeDtypeStruct((members, reflections_n, share, detector), jnp.bfloat16),
        ],
        scratch_shapes=[
            pltpu.VMEM((tile * reflections_n, detector), jnp.float32),
            pltpu.VMEM((rows, wide_n), jnp.float32),
        ],
        compiler_params=pltpu.CompilerParams(vmem_limit_bytes=12 * 2**20),
        name="forward",
    )(band_start, band_len, volume, rays)
    block = (reflections_n, share, detector)
    masked, residual = pl.pallas_call(
        lambda *refs: exchange_kernel(n, *refs),
        in_specs=[smem, smem, smem, vmem, vmem],
        out_specs=[vmem, vmem],
        out_shape=[
            jax.ShapeDtypeStruct((rows, wide_n), jnp.bfloat16),
            jax.ShapeDtypeStruct((rows, detector), jnp.float32),
        ],
        scratch_shapes=[
            pltpu.VMEM((members, share, detector), jnp.bfloat16),
            pltpu.VMEM((members - 1,) + block, jnp.bfloat16),
            pltpu.VMEM((n, share, detector), jnp.bfloat16),
            pltpu.VMEM((members,) + block, jnp.bfloat16),
            pltpu.VMEM((FRAMES - 1, members, share, detector), jnp.bfloat16),
            pltpu.VMEM((FRAMES, members, share, detector), jnp.bfloat16),
            pltpu.SemaphoreType.DMA((n,)),
            pltpu.SemaphoreType.DMA((n,)),
            pltpu.SemaphoreType.DMA((members - 1,)),
            pltpu.SemaphoreType.DMA((members - 1,)),
            pltpu.SemaphoreType.DMA((members - 1,)),
            pltpu.SemaphoreType.DMA((members - 1,)),
            pltpu.SemaphoreType.DMA((FRAMES - 1,)),
            pltpu.SemaphoreType.DMA((FRAMES - 1,)),
        ],
        compiler_params=pltpu.CompilerParams(
            collective_id=0, has_side_effects=True, vmem_limit_bytes=4 * 2**20
        ),
        name="exchange",
    )(band_start, band_len, slot_image, contrib, measured.reshape(members, share, detector))
    step_gain = math.sqrt(cell_count * n / (FRAMES * reflections_n * detector))
    updated = pl.pallas_call(
        functools.partial(backward_kernel, step_gain),
        grid=(cell_count // tile,),
        in_specs=[
            smem,
            pl.BlockSpec((rows, tile), lambda c: (0, c)),
            pl.BlockSpec((tile, wide_n), lambda c: (c, 0)),
            pl.BlockSpec((rows, wide_n), lambda c: (0, 0)),
        ],
        out_specs=pl.BlockSpec((rows, tile), lambda c: (0, c)),
        out_shape=jax.ShapeDtypeStruct((rows, cell_count), jnp.bfloat16),
        compiler_params=pltpu.CompilerParams(vmem_limit_bytes=12 * 2**20),
        name="backward",
    )(relax, volume, flat, masked)
    return updated[None], residual[None]


def chosen(*operands):
    volume, rays, _, _, slot_image, measured, _ = operands
    n = lax.axis_size("orient")
    plain = (
        lax.axis_size("slab") == 1
        and volume.shape[0] == 1
        and measured.shape[0] == 1
        and n % FRAMES == 0
        and n > FRAMES
        and volume.shape[1] % (16 * (n // FRAMES)) == 0
        and volume.shape[2] % min(512, volume.shape[2]) == 0
        and rays.shape[1] % 8 == 0
        and rays.shape[2] % 128 == 0
    )
    return fast(*operands) if plain else local(*operands)


def solution(mesh):
    placed = (
        P("orient", "slab", None),
        P(),
        P(None, "orient"),
        P(None, "orient"),
        P(),
        P("orient", "slab", None),
        P("orient"),
    )
    return jax.shard_map(
        chosen,
        mesh=mesh,
        in_specs=placed,
        out_specs=(P("orient", "slab", None), P("orient", "slab", None)),
        check_vma=False,
    )
```
